32 devices in a mesh: near: 4 (over x, core), off: 8 (over z, y).
Axes of the slice: x: 2, y: 2, z: 4, core: 2. Of those that a mesh axis runs over, the one named last changes fastest.
Arguments:
- adjoint: float32 [64, 128, 6, 128], P('near', 'off'), may hold values from -6 to 6
- jacobian: bfloat16 [64, 128, 7, 36, 128], P('near', 'off'), may hold values from -1 to 1
- source: float32 [64, 128, 6, 128], P('near', 'off'), may hold values from -4 to 4
- pseudo_step: float32 [64, 128, 128], P('near', 'off'), may hold values from 0.05 to 0.5
- receptor_count: int32 [32], P(('near', 'off')), may hold values from 512 to 1024, as said below
- receptor_cell: int32 [32768], P(('near', 'off')), may hold values from 0 to 32767
- donor_owner: int32 [32768, 1], P(('near', 'off')), may hold values from 0 to 31; in each aligned block of 1024 rows (0 to 1023, 1024 to 2047, ...) at most 48 rows name the same one
- donor_base: int32 [32768], P(('near', 'off')), may hold values from 0 to 30590, as said below
- donor_fraction: float32 [32768, 3], P(('near', 'off')), may hold values from 0 to 1
Outputs:
- residual: float32 [64, 128, 6, 128], P('near', 'off')
- updated: float32 [64, 128, 6, 128], P('near', 'off')
The draws below stay inside these ranges and needn't reach their ends.
Inputs may be any that keep to these rules, and one draw needn't show every extreme that they name: `receptor_count`: A multiple of 128; rows of a block at or above its count are padding. `donor_owner`: among the 1024 rows of one block, padding included, at most 48 name the same owner block. `donor_base`: the donor cube lies inside the owner block: its lowest corner has ix < 15, iy < 15, iz < 127.
All inputs are finite; a program needn't handle non-finite values.
Results may differ from the reference program's by a relative error of at most 0.0025.
Values may be sent and summed in bfloat16 or wider, within the bound.
A program may use at most 192 MiB of HBM per device.

```python
import math
import jax
import jax.numpy as jnp
import numpy as np
from jax import lax

NVAR = 6
CX = 16
CY = 16
CZ = 128
REC_DEV = 1024
NX = 64
NY = 128
BLOCKS = 32
RECEPTORS = 32768
CAP = 48
N_OFF = 8


def draw_receptor_count(key, part):
    lowest = max(1, REC_DEV // 256)
    highest = REC_DEV // 128
    key_one, key_two = jax.random.split(key)
    multiple = jax.random.randint(key_one, (BLOCKS,), lowest, highest + 1)
    counts = multiple * 128
    chosen = jax.random.randint(key_two, (), 0, BLOCKS)
    counts = counts.at[chosen].set(REC_DEV)
    counts = counts.at[(chosen + 1) % BLOCKS].set(128 * lowest)
    return counts.astype(jnp.int32)


def draw_donor_base(key, part):
    key_x, key_y, key_z = jax.random.split(key, 3)
    cell_x = jax.random.randint(key_x, (RECEPTORS,), 0, CX - 1)
    cell_y = jax.random.randint(key_y, (RECEPTORS,), 0, CY - 1)
    cell_z = jax.random.randint(key_z, (RECEPTORS,), 0, CZ - 1)
    flat_index = (cell_x * CY + cell_y) * CZ + cell_z
    flat_index = flat_index.at[0].set(((CX - 2) * CY + CY - 2) * CZ + CZ - 2)
    flat_index = flat_index.at[1].set(0)
    return flat_index.astype(jnp.int32)


def with_ends(entries, stream_key, least, top_value):
    longest = entries.shape.index(max(entries.shape))
    spots = []
    for shift in (0, 1):
        where = [jax.random.randint(jax.random.fold_in(stream_key, axis), (), 0, length) for axis, length in enumerate(entries.shape)]
        where[longest] = (where[longest] + shift) % entries.shape[longest]
        spots.append(tuple(where))
    return entries.at[spots[0]].set(least).at[spots[1]].set(top_value)


def steps_of(key, dims, cuts, least, high):
    gain, own = 1.0, jax.random.fold_in(key, 6)
    for axis_at, blocks in cuts:
        steps = jnp.exp(jax.random.uniform(jax.random.fold_in(own, axis_at), (blocks,), jnp.float32, least / len(cuts), high / len(cuts)))
        gain = gain * jnp.repeat(steps, dims[axis_at] // blocks).reshape([-1 if axis == axis_at else 1 for axis in range(len(dims))])
    return gain


def shared_out(rng, own, number, rows, count, top, reach, lean):
    order = jax.random.permutation(rng, count)
    packed, usual = portions_of(count, rows * top, reach, lean, True), portions_of(count, rows * top, reach, lean, False)
    places = jnp.arange(count)

    def named(lengths, turn):
        used = int((lengths > 0).sum())
        fixed = max(1, used // 4)
        passed = fixed + (places - fixed + turn * (used - fixed)) % max(1, count - fixed)
        return jnp.zeros((count,), jnp.int32).at[order[jnp.where(places < fixed, places, passed)]].set(jnp.asarray(lengths, jnp.int32))

    lengths = jnp.where(number % 4 == 0, named(packed, number // 4), named(usual, number - number // 4 - 1))
    mixed = jax.random.permutation(jax.random.fold_in(own, 3), count)
    giver, sink = mixed[0:count // 2 * 2:2], mixed[1:count // 2 * 2:2]
    room = jnp.minimum(lengths[giver] - 1, reach - lengths[sink]) // 2
    room = jnp.where((giver == order[0]) | (sink == order[0]) | (lengths[sink] == 0), 0, jnp.maximum(room, 0))
    passed = jax.random.randint(jax.random.fold_in(own, 4), (count // 2,), 0, 1 << 20) % (room + 1)
    lengths = lengths.at[giver].add(-passed).at[sink].add(passed)
    items = jnp.searchsorted(jnp.cumsum(lengths), jnp.arange(rows * top), side="right").astype(jnp.int32)
    grid = items.reshape(top, rows).T
    grid = grid[jax.random.permutation(jax.random.fold_in(own, 1), rows)]
    turn = jax.random.randint(jax.random.fold_in(own, 2), (rows, 1), 0, top)
    return jnp.take_along_axis(grid, (jnp.arange(top)[None, :] + turn) % top, axis=1)


def portions_of(number_of, total, limit, skew, full):
    portions = [(1 << 20) // math.isqrt(rank ** skew) + 1 for rank in range(1, number_of + 1)]
    largest = limit if full else min(limit, max(-(-total // number_of), total * portions[0] // sum(portions)))
    least = 1 if total - largest >= number_of - 1 else 0
    given, rest = [largest] + [least] * (number_of - 1), total - largest - least * (number_of - 1)
    while rest > 0:
        free = [i for i in range(1, number_of) if given[i] < largest] or [i for i in range(1, number_of) if given[i] < limit]
        mass, left = sum([portions[i] for i in free]), rest
        for i in free:
            more = min(limit - given[i], max(1, left * portions[i] // mass), rest)
            given[i] = given[i] + more
            rest = rest - more
    return np.array(given)


def scatter_about(stream_key, extent, scale, most, cuts=(), kind=jnp.bfloat16):
    values = scale * jax.random.normal(stream_key, extent, jnp.float32)
    if cuts:
        values = values * steps_of(stream_key, extent, cuts, -0.22, 0.18)
    return jnp.clip(values, -most, most).astype(kind)


def setup_inputs(seed: int = 0) -> dict:
    key_list = jax.random.split(jax.random.key(seed), 10)
    adjoint = scatter_about(key_list[0], (NX, NY, NVAR, CZ), 1.0, 6.0, ((0, 4), (1, 8)), jnp.float32)
    jacobian = scatter_about(key_list[1], (NX, NY, 7, NVAR * NVAR, CZ), (7 * NVAR) ** -0.5, 1.0, ((0, 4), (1, 8)))
    source = scatter_about(key_list[2], (NX, NY, NVAR, CZ), 0.5, 4.0, ((0, 4), (1, 8)), jnp.float32)
    pseudo_step = jnp.clip(jnp.exp(math.log(0.5) - 2.3025851 * jax.random.uniform(key_list[3], (NX, NY, CZ), jnp.float32) ** steps_of(key_list[3], (NX, NY, CZ), ((0, 4), (1, 8)), -0.2, 0.2)), 0.05, 0.5)
    receptor_count = draw_receptor_count(jax.random.fold_in(key_list[9], 71), 0)
    receptor_cell = with_ends(jax.random.randint(key_list[5], (RECEPTORS,), 0, CX * CY * CZ), jax.random.fold_in(key_list[5], 1), 0, (CX * CY * CZ) - 1).astype(jnp.int32)
    donor_owner_keys = jax.random.split(jax.random.fold_in(key_list[6], 1), RECEPTORS // REC_DEV)
    donor_owner_turns = jax.random.permutation(jax.random.fold_in(key_list[6], 3), RECEPTORS // REC_DEV)
    donor_owner = jax.vmap(lambda own, number: shared_out(jax.random.fold_in(key_list[6], 2), own, number, REC_DEV, BLOCKS, 1, CAP, 2))(donor_owner_keys, donor_owner_turns).reshape((RECEPTORS, 1))
    donor_base = draw_donor_base(jax.random.fold_in(key_list[9], 71), 0)
    donor_fraction = jnp.clip(1.0 * jax.random.uniform(key_list[8], (RECEPTORS, 3), jnp.float32) ** steps_of(key_list[8], (RECEPTORS, 3), ((0, 32),), -0.2, 0.2), 0.0, 1.0)
    return {"adjoint": adjoint, "jacobian": jacobian, "source": source, "pseudo_step": pseudo_step, "receptor_count": receptor_count, "receptor_cell": receptor_cell, "donor_owner": donor_owner, "donor_base": donor_base, "donor_fraction": donor_fraction}


OFFSETS = ((0, 0, 0), (1, 0, 0), (-1, 0, 0), (0, 1, 0), (0, -1, 0), (0, 0, 1), (0, 0, -1))
CORNERS = tuple(((corner >> 2) & 1, (corner >> 1) & 1, corner & 1) for corner in range(8))


def moved(field, offset, axis):
    if offset == 0:
        return field
    length = field.shape[axis]
    widths = [(0, 0)] * field.ndim
    if offset > 0:
        widths[axis] = (1, 0)
        return lax.slice_in_dim(jnp.pad(field, widths), 0, length, axis=axis)
    widths[axis] = (0, 1)
    return lax.slice_in_dim(jnp.pad(field, widths), 1, length + 1, axis=axis)


def factor(fraction, chosen):
    if chosen == 1:
        return fraction
    return 1.0 - fraction


def reference(adjoint, jacobian, source, pseudo_step, receptor_count, receptor_cell, donor_owner, donor_base, donor_fraction):
    adjoint_low = lax.optimization_barrier(adjoint.astype(jnp.bfloat16))
    values = adjoint_low.astype(jnp.float32)
    flux = jnp.zeros(adjoint.shape, jnp.float32)
    for stencil in range(7):
        shift_x, shift_y, shift_z = OFFSETS[stencil]
        blocks = jacobian[:, :, stencil].astype(jnp.float32).reshape(NX, NY, NVAR, NVAR, CZ)
        product = jnp.einsum("xyabz,xyaz->xybz", blocks, values, precision=lax.Precision.HIGHEST)
        product = moved(moved(moved(product, shift_x, 0), shift_y, 1), shift_z, 3)
        flux = flux + product
    row_index = jnp.arange(RECEPTORS, dtype=jnp.int32)
    sender = row_index // REC_DEV
    live = (row_index % REC_DEV) < receptor_count[sender]
    cell_x = (sender // N_OFF) * CX + receptor_cell // (CY * CZ)
    cell_y = (sender % N_OFF) * CY + (receptor_cell // CZ) % CY
    cell_z = receptor_cell % CZ
    rows_mu = jnp.where(live[:, None], values[cell_x, cell_y, :, cell_z], 0.0)
    owner = donor_owner[:, 0]
    donor_x = (owner // N_OFF) * CX + donor_base // (CY * CZ)
    donor_y = (owner % N_OFF) * CY + (donor_base // CZ) % CY
    donor_z = donor_base % CZ
    total = flux
    for offset_x, offset_y, offset_z in CORNERS:
        weight = factor(donor_fraction[:, 0], offset_x) * factor(donor_fraction[:, 1], offset_y) * factor(donor_fraction[:, 2], offset_z)
        total = total.at[donor_x + offset_x, donor_y + offset_y, :, donor_z + offset_z].add(-weight[:, None] * rows_mu)
    residual = total + source
    updated = adjoint - pseudo_step[:, :, None, :] * residual
    return residual, updated
```

```python
import functools

import jax
import jax.numpy as jnp
from jax import lax
from jax.experimental import pallas as pl
from jax.experimental.pallas import tpu as pltpu
from jax.sharding import PartitionSpec as P

F32 = jnp.float32
BF16 = jnp.bfloat16
VMEM_LIMIT = 58 * 1024 * 1024
NT = (((1,), (1,)), ((), ()))


def fold(product, var_count):
    total = product[..., 0:var_count, :]
    for a in range(1, var_count):
        total = total + product[..., a * var_count : (a + 1) * var_count, :]
    return total


def spread_adjoint(adj_ref, wide_ref):
    size_x, size_y, var_count, size_z = adj_ref.shape
    rows = var_count * var_count
    side = jnp.zeros((size_y + 2, rows, size_z), F32)
    wide_ref[0] = side
    wide_ref[size_x + 1] = side
    edge = jnp.zeros((rows, size_z), F32)

    def plane(x, carry):
        wide_ref[x + 1, 0] = edge
        wide_ref[x + 1, size_y + 1] = edge
        low = adj_ref[x].astype(BF16).astype(F32)
        for a in range(var_count):
            wide_ref[x + 1, 1 : size_y + 1, a * var_count : (a + 1) * var_count, :] = jnp.broadcast_to(
                low[:, a : a + 1, :], (size_y, var_count, size_z)
            )
        return carry

    lax.fori_loop(0, size_x, plane, 0)


def pack_rows(count_ref, cell_ref, owner_ref, base_ref, frac_ref, adj_ref, padded_ref, masked_ref, me, blocks, stride):
    size_x, size_y, var_count, size_z = adj_ref.shape
    rows = cell_ref.shape[1]
    lanes = 128
    z_bits = size_z.bit_length() - 1
    row = lax.broadcasted_iota(jnp.int32, (1, rows), 1)
    live = row < count_ref[0]
    cell = cell_ref[...]
    cell_z = cell & (size_z - 1)
    cell_xy = cell >> z_bits
    hot_z = jnp.where(lax.broadcasted_iota(jnp.int32, (size_z, rows), 0) == cell_z, 1.0, 0.0).astype(BF16)
    padded_ref[:, var_count:8, :] = jnp.zeros((size_y, 8 - var_count, size_z), F32)

    def gather(x, mu):
        padded_ref[:, 0:var_count, :] = adj_ref[x]
        plane = padded_ref[...].reshape(size_y * 8, size_z).astype(BF16)
        picked = jnp.dot(plane, hot_z, preferred_element_type=F32)
        for y in range(size_y):
            mu = jnp.where(cell_xy == x * size_y + y, picked[y * 8 : y * 8 + 8], mu)
        return mu

    mu = lax.fori_loop(0, size_x, gather, jnp.zeros((8, rows), F32))
    base = base_ref[...]
    base_xy = (base >> z_bits).astype(F32)
    base_z = (base & (size_z - 1)).astype(F32)
    sub = lax.broadcasted_iota(jnp.int32, (8, rows), 0)
    top = jnp.where(sub < var_count, mu, jnp.where(sub == var_count, base_xy, base_z))
    frac = frac_ref[...]
    frac_hi = frac.astype(BF16).astype(F32)
    payload = jnp.concatenate([top, frac_hi, frac - frac_hi], axis=0)
    owner = jnp.where(live, owner_ref[...], -1)

    strips = rows // lanes
    block_ids = lax.broadcasted_iota(jnp.int32, (blocks, lanes), 0)
    matches = [
        jnp.where(block_ids == owner[:, s * lanes : (s + 1) * lanes], 1.0, 0.0) for s in range(strips)
    ]
    before = jnp.where(
        lax.broadcasted_iota(jnp.int32, (lanes, lanes), 0) < lax.broadcasted_iota(jnp.int32, (lanes, lanes), 1), 1.0, 0.0
    ).astype(BF16)
    earlier = jnp.dot(jnp.concatenate(matches, axis=0).astype(BF16), before, preferred_element_type=F32)
    carry = jnp.zeros((blocks, 1), F32)
    ranks = []
    for s in range(strips):
        here = earlier[s * blocks : (s + 1) * blocks] + carry
        ranks.append(jnp.sum(here * matches[s], axis=0, keepdims=True))
        carry = carry + jnp.sum(matches[s], axis=1, keepdims=True)
    rank = jnp.concatenate(ranks, axis=1).astype(jnp.int32)
    place = rank + lax.rem(me, lanes // stride) * stride
    hot_rank = jnp.where(lax.broadcasted_iota(jnp.int32, (lanes, rows), 0) == place, 1.0, 0.0).astype(BF16)

    def mask(o, carry):
        masked_ref[pl.ds(pl.multiple_of(o * 16, 16), 16), :] = jnp.where(owner == o, payload, 0.0).astype(BF16)
        return carry

    lax.fori_loop(0, blocks, mask, 0)
    return lax.dot_general(masked_ref[...], hot_rank, NT, preferred_element_type=F32).astype(BF16)


def pack_kernel(blocks, stride, off_count, count_ref, cell_ref, owner_ref, base_ref, frac_ref, adj_ref, jac_ref,
                tiles_ref, rims_ref, wide_ref, rim_ref, padded_ref, masked_ref, sems):
    size_x, size_y, var_count, size_z = adj_ref.shape
    me = lax.axis_index("near") * off_count + lax.axis_index("off")
    sources = (
        jac_ref.at[size_x - 1, :, 1],
        jac_ref.at[0, :, 2],
        jac_ref.at[:, size_y - 1, 3],
        jac_ref.at[:, 0, 4],
    )
    copies = [pltpu.make_async_copy(s, rim_ref.at[i], sems.at[i]) for i, s in enumerate(sources)]
    for copy in copies:
        copy.start()
    spread_adjoint(adj_ref, wide_ref)
    tiles = pack_rows(count_ref, cell_ref, owner_ref, base_ref, frac_ref, adj_ref, padded_ref, masked_ref, me, blocks, stride)
    tiles_ref[...] = tiles.reshape(blocks, 16, 128)
    for copy in copies:
        copy.wait()
    rims_ref[0] = fold(rim_ref[0].astype(F32) * wide_ref[size_x, 1 : size_y + 1], var_count)
    rims_ref[1] = fold(rim_ref[1].astype(F32) * wide_ref[1, 1 : size_y + 1], var_count)
    rims_ref[2] = fold(rim_ref[2].astype(F32) * wide_ref[1 : size_x + 1, size_y], var_count)
    rims_ref[3] = fold(rim_ref[3].astype(F32) * wide_ref[1 : size_x + 1, 1], var_count)


def flux_planes(adj_shape, jac_hbm, jac_ref, wide_ref, flux_ref, sems):
    size_x, size_y, var_count, size_z = adj_shape

    def copy(x):
        return pltpu.make_async_copy(jac_hbm.at[x], jac_ref.at[x], sems.at[x])

    lane = lax.broadcasted_iota(jnp.int32, (var_count, size_z), 1)

    copy(0).wait()

    def plane(x, carry):
        @pl.when(x + 1 < size_x)
        def _():
            copy(x + 1).wait()

        lower = jnp.maximum(x - 1, 0)
        upper = jnp.minimum(x + 1, size_x - 1)

        def column(y, carry):
            left = jnp.maximum(y - 1, 0)
            right = jnp.minimum(y + 1, size_y - 1)
            mine = wide_ref[x + 1, y + 1]
            here = jac_ref[x, y, 0].astype(F32) * mine
            here += jac_ref[lower, y, 1].astype(F32) * wide_ref[x, y + 1]
            here += jac_ref[upper, y, 2].astype(F32) * wide_ref[x + 2, y + 1]
            here += jac_ref[x, left, 3].astype(F32) * wide_ref[x + 1, y]
            here += jac_ref[x, right, 4].astype(F32) * wide_ref[x + 1, y + 2]
            total = fold(here, var_count)
            up = fold(jac_ref[x, y, 5].astype(F32) * mine, var_count)
            down = fold(jac_ref[x, y, 6].astype(F32) * mine, var_count)
            total += jnp.where(lane == 0, 0.0, pltpu.roll(up, 1, 1))
            total += jnp.where(lane == size_z - 1, 0.0, pltpu.roll(down, size_z - 1, 1))
            flux_ref[x, y] = total
            return carry

        lax.fori_loop(0, size_y, column, 0, unroll=4)
        return carry

    lax.fori_loop(0, size_x, plane, 0)


def overset_factors(recv_ref, stride, size_x, size_y, size_z, var_count):
    blocks = recv_ref.shape[0]
    group = 128 // stride
    mus, wxs, wys, wzs = [], [], [], []
    y_bits = size_y.bit_length() - 1

    def hat(index, fraction, length):
        at = lax.broadcasted_iota(jnp.int32, (length, 128), 0)
        return jnp.where(at == index, 1.0 - fraction, jnp.where(at == index + 1, fraction, 0.0))

    for g in range(blocks // group):
        tile = recv_ref[g * group].astype(F32)
        for i in range(1, group):
            tile = tile + recv_ref[g * group + i].astype(F32)
        frac = tile[8:12] + tile[12:16]
        xy = tile[var_count : var_count + 1].astype(jnp.int32)
        z = tile[var_count + 1 : var_count + 2].astype(jnp.int32)
        mus.append(-tile[0:8])
        wxs.append(hat(xy >> y_bits, frac[0:1], size_x))
        wys.append(hat(xy & (size_y - 1), frac[1:2], size_y))
        wzs.append(hat(z, frac[2:3], size_z))
    return tuple(jnp.concatenate(part, axis=1) for part in (mus, wxs, wys, wzs))


def finish_kernel(stride, adj_ref, src_ref, step_ref, recv_ref, rim_xl, rim_xh, rim_yl, rim_yh, jac_hbm,
                  res_ref, upd_ref, jac_ref, wide_ref, wx_ref, wy_ref, wz_ref, left_ref, sems):
    size_x, size_y, var_count, size_z = adj_ref.shape

    def start(x, carry):
        pltpu.make_async_copy(jac_hbm.at[x], jac_ref.at[x], sems.at[x]).start()
        return carry

    lax.fori_loop(0, size_x, start, 0)
    spread_adjoint(adj_ref, wide_ref)
    mu, wx, wy, wz = overset_factors(recv_ref, stride, size_x, size_y, size_z, var_count)
    wx_ref[...] = wx
    wy_ref[...] = wy
    wz_hi = wz.astype(BF16)
    wz_ref[0] = wz_hi
    wz_ref[1] = (wz - wz_hi.astype(F32)).astype(BF16)
    flux_planes(adj_ref.shape, jac_hbm, jac_ref, wide_ref, res_ref, sems)
    res_ref[0] += rim_xl[...]
    res_ref[size_x - 1] += rim_xh[...]
    res_ref[:, 0] += rim_yl[...]
    res_ref[:, size_y - 1] += rim_yh[...]

    def plane(x, carry):
        mux = mu * wx_ref[pl.ds(x, 1), :]
        for y in range(0, size_y, 2):
            pair = jnp.concatenate([mux * wy_ref[y : y + 1, :], mux * wy_ref[y + 1 : y + 2, :]], axis=0)
            left_ref[y * 8 : y * 8 + 16, :] = pair.astype(BF16)
        left = left_ref[...]
        over = lax.dot_general(left, wz_ref[0], NT, preferred_element_type=F32)
        over += lax.dot_general(left, wz_ref[1], NT, preferred_element_type=F32)
        over = over.reshape(size_y, 8, size_z)[:, 0:var_count, :]
        res = res_ref[x] + over + src_ref[x]
        res_ref[x] = res
        upd_ref[x] = adj_ref[x] - step_ref[x][:, None, :] * res
        return carry

    lax.fori_loop(0, size_x, plane, 0)


def passed_along(block, axis, distance):
    devices = range(lax.axis_size(axis))
    route = [(i - distance, i) for i in devices if i - distance in devices]
    return lax.ppermute(block, axis, route)


def shards(adjoint, jacobian, source, pseudo_step, receptor_count, receptor_cell, donor_owner, donor_base, donor_fraction):
    size_x, size_y, var_count, size_z = adjoint.shape
    rows = var_count * var_count
    off_count = lax.axis_size("off")
    blocks = lax.axis_size("near") * off_count
    row_count = receptor_cell.shape[0]
    capacity = max(2, 3 * row_count // (2 * blocks))
    stride = 1 << (capacity - 1).bit_length()
    slots = blocks * stride
    vmem = pl.BlockSpec(memory_space=pltpu.VMEM)
    hbm = pl.BlockSpec(memory_space=pl.ANY)
    frac = jnp.pad(donor_fraction.T, ((0, 1), (0, 0)))
    tiles, rims = pl.pallas_call(
        functools.partial(pack_kernel, blocks, stride, off_count),
        out_shape=(
            jax.ShapeDtypeStruct((blocks, 16, 128), BF16),
            jax.ShapeDtypeStruct((4, size_y, var_count, size_z), F32),
        ),
        in_specs=[pl.BlockSpec(memory_space=pltpu.SMEM)] + [vmem] * 5 + [hbm],
        out_specs=(vmem, vmem),
        scratch_shapes=[
            pltpu.VMEM((size_x + 2, size_y + 2, rows, size_z), F32),
            pltpu.VMEM((4, size_y, rows, size_z), BF16),
            pltpu.VMEM((size_y, 8, size_z), F32),
            pltpu.VMEM((blocks * 16, row_count), BF16),
            pltpu.SemaphoreType.DMA((4,)),
        ],
        compiler_params=pltpu.CompilerParams(vmem_limit_bytes=VMEM_LIMIT),
    )(
        receptor_count,
        receptor_cell.reshape(1, row_count),
        donor_owner.reshape(1, row_count),
        donor_base.reshape(1, row_count),
        frac,
        adjoint,
        jacobian,
    )
    received = lax.all_to_all(tiles, ("near", "off"), split_axis=0, concat_axis=0, tiled=True)
    rim_xl = passed_along(rims[0], "near", 1)
    rim_xh = passed_along(rims[1], "near", -1)
    rim_yl = passed_along(rims[2], "off", 1)
    rim_yh = passed_along(rims[3], "off", -1)
    return tuple(
        pl.pallas_call(
            functools.partial(finish_kernel, stride),
            out_shape=(jax.ShapeDtypeStruct(adjoint.shape, F32), jax.ShapeDtypeStruct(adjoint.shape, F32)),
            in_specs=[vmem] * 8 + [hbm],
            out_specs=(vmem, vmem),
            scratch_shapes=[
                pltpu.VMEM(jacobian.shape, BF16),
                pltpu.VMEM((size_x + 2, size_y + 2, rows, size_z), F32),
                pltpu.VMEM((size_x, slots), F32),
                pltpu.VMEM((size_y, slots), F32),
                pltpu.VMEM((2, size_z, slots), BF16),
                pltpu.VMEM((size_y * 8, slots), BF16),
                pltpu.SemaphoreType.DMA((size_x,)),
            ],
            compiler_params=pltpu.CompilerParams(vmem_limit_bytes=VMEM_LIMIT),
        )(adjoint, source, pseudo_step, received, rim_xl, rim_xh, rim_yl, rim_yh, jacobian)
    )


def solution(mesh):
    in_specs = (
        P("near", "off", None, None),
        P("near", "off", None, None, None),
        P("near", "off", None, None),
        P("near", "off", None),
        P(("near", "off")),
        P(("near", "off")),
        P(("near", "off"), None),
        P(("near", "off")),
        P(("near", "off"), None),
    )
    out_specs = (P("near", "off", None, None), P("near", "off", None, None))
    return jax.shard_map(shards, mesh=mesh, in_specs=in_specs, out_specs=out_specs, check_vma=False)
```

```python
import functools

import jax
import jax.numpy as jnp
from jax import lax
from jax.experimental import pallas as pl
from jax.experimental.pallas import tpu as pltpu
from jax.sharding import PartitionSpec as P

F32 = jnp.float32
BF16 = jnp.bfloat16
VMEM_LIMIT = 56 * 1024 * 1024
NT = (((1,), (1,)), ((), ()))
MESH = pl.DeviceIdType.MESH
LANES = 128


def contracted(blocks, values, b):
    var_count = len(values)
    total = blocks(b).astype(F32) * values[0]
    for a in range(1, var_count):
        total += blocks(a * var_count + b).astype(F32) * values[a]
    return total


def low_of(adj_ref, x):
    return [adj_ref[x, a].astype(BF16).astype(F32) for a in range(adj_ref.shape[1])]


def pack_rows(count_ref, cell_ref, owner_ref, base_ref, frac_ref, adj_ref, masked_ref, picked_ref, me, blocks, stride):
    size_x, var_count, size_y, size_z = adj_ref.shape
    rows = cell_ref.shape[1]
    z_bits = size_z.bit_length() - 1
    row = lax.broadcasted_iota(jnp.int32, (1, rows), 1)
    live = row < count_ref[0]
    cell = cell_ref[...]
    cell_z = cell & (size_z - 1)
    cell_xy = cell >> z_bits
    hot_z = jnp.where(lax.broadcasted_iota(jnp.int32, (size_z, rows), 0) == cell_z, 1.0, 0.0).astype(BF16)
    picked_ref[...] = jnp.zeros(picked_ref.shape, F32)
    y_of = lax.broadcasted_iota(jnp.int32, (size_y, rows), 0)

    def gather(x, carry):
        plane = adj_ref[x].reshape(var_count * size_y, size_z).astype(BF16)
        found = jnp.dot(plane, hot_z, preferred_element_type=F32)
        here = y_of == cell_xy - x * size_y
        for a in range(var_count):
            at = slice(a * size_y, (a + 1) * size_y)
            picked_ref[at, :] = jnp.where(here, found[at], picked_ref[at, :])
        return carry

    lax.fori_loop(0, size_x, gather, 0)
    base = base_ref[...]
    base_xy = (base >> z_bits).astype(F32)
    base_z = (base & (size_z - 1)).astype(F32)
    sub = lax.broadcasted_iota(jnp.int32, (8, rows), 0)
    top = jnp.where(sub == var_count, base_xy, base_z)
    for a in range(var_count):
        mu = jnp.sum(picked_ref[a * size_y : (a + 1) * size_y, :], axis=0, keepdims=True)
        top = jnp.where(sub == a, mu, top)
    frac = frac_ref[...]
    frac_hi = frac.astype(BF16).astype(F32)
    payload = jnp.concatenate([top, frac_hi, frac - frac_hi], axis=0)
    owner = jnp.where(live, owner_ref[...], -1)

    strips = rows // LANES
    block_ids = lax.broadcasted_iota(jnp.int32, (blocks, LANES), 0)
    matches = [
        jnp.where(block_ids == owner[:, s * LANES : (s + 1) * LANES], 1.0, 0.0) for s in range(strips)
    ]
    first = lax.broadcasted_iota(jnp.int32, (LANES, LANES), 0)
    second = lax.broadcasted_iota(jnp.int32, (LANES, LANES), 1)
    before = jnp.where(first < second, 1.0, 0.0).astype(BF16)
    earlier = jnp.dot(jnp.concatenate(matches, axis=0).astype(BF16), before, preferred_element_type=F32)
    carry = jnp.zeros((blocks, 1), F32)
    ranks = []
    for s in range(strips):
        here = earlier[s * blocks : (s + 1) * blocks] + carry
        ranks.append(jnp.sum(here * matches[s], axis=0, keepdims=True))
        carry = carry + jnp.sum(matches[s], axis=1, keepdims=True)
    rank = jnp.concatenate(ranks, axis=1).astype(jnp.int32)
    place = rank + lax.rem(me, LANES // stride) * stride
    hot_rank = jnp.where(lax.broadcasted_iota(jnp.int32, (LANES, rows), 0) == place, 1.0, 0.0).astype(BF16)

    def mask(o, carry):
        masked_ref[pl.ds(pl.multiple_of(o * 16, 16), 16), :] = jnp.where(owner == o, payload, 0.0).astype(BF16)
        return carry

    lax.fori_loop(0, blocks, mask, 0)
    return lax.dot_general(masked_ref[...], hot_rank, NT, preferred_element_type=F32).astype(BF16)


def start_side(jac_hbm, side_ref, edge_ref, sems):
    size_x = jac_hbm.shape[0]
    copies = [
        pltpu.make_async_copy(jac_hbm.at[size_x - 1, 1], edge_ref.at[0], sems.at[0]),
        pltpu.make_async_copy(jac_hbm.at[0, 2], edge_ref.at[1], sems.at[1]),
        pltpu.make_async_copy(jac_hbm.at[:, pl.ds(3, 2)], side_ref, sems.at[2]),
    ]
    for copy in copies:
        copy.start()
    return copies


def side_flux(copies, adj_ref, side_ref, edge_ref, rimx_ref, rimy_ref, part_ref):
    size_x, var_count, size_y, size_z = adj_ref.shape
    for copy in copies:
        copy.wait()
    for i, x in enumerate((size_x - 1, 0)):
        low = low_of(adj_ref, x)
        for b in range(var_count):
            rimx_ref[i, b] = contracted(lambda n: edge_ref[i, n], low, b)
    y_of = lax.broadcasted_iota(jnp.int32, (size_y, size_z), 0)

    def plane(x, carry):
        low = low_of(adj_ref, x)
        for b in range(var_count):
            up = pltpu.roll(contracted(lambda n: side_ref[x, 0, n], low, b), 1, 0)
            down = pltpu.roll(contracted(lambda n: side_ref[x, 1, n], low, b), size_y - 1, 0)
            rimy_ref[0, x, b : b + 1, :] = up[0:1]
            rimy_ref[1, x, b : b + 1, :] = down[size_y - 1 : size_y]
            part_ref[x, b] = jnp.where(y_of == 0, 0.0, up) + jnp.where(y_of == size_y - 1, 0.0, down)
        return carry

    lax.fori_loop(0, size_x, plane, 0)


def plane_copies(jac_hbm, jac_ref, sems, x):
    return (
        pltpu.make_async_copy(jac_hbm.at[x, pl.ds(0, 3)], jac_ref.at[x, pl.ds(0, 3)], sems.at[x, 0]),
        pltpu.make_async_copy(jac_hbm.at[x, pl.ds(5, 2)], jac_ref.at[x, pl.ds(3, 2)], sems.at[x, 1]),
    )


def start_planes(jac_hbm, jac_ref, sems):
    def start(x, carry):
        for copy in plane_copies(jac_hbm, jac_ref, sems, x):
            copy.start()
        return carry

    lax.fori_loop(0, jac_hbm.shape[0], start, 0)


def main_flux(adj_ref, jac_hbm, jac_ref, low_ref, part_ref, flux_ref, sems):
    size_x, var_count, size_y, size_z = adj_ref.shape
    low_ref[0] = jnp.zeros(low_ref.shape[1:], F32)
    low_ref[size_x + 1] = jnp.zeros(low_ref.shape[1:], F32)

    def narrow(x, carry):
        low_ref[x + 1] = adj_ref[x].astype(BF16).astype(F32)
        return carry

    lax.fori_loop(0, size_x, narrow, 0)
    lane = lax.broadcasted_iota(jnp.int32, (size_y, size_z), 1)

    def wait(x):
        for copy in plane_copies(jac_hbm, jac_ref, sems, x):
            copy.wait()

    wait(0)

    def plane(x, carry):
        @pl.when(x + 1 < size_x)
        def _():
            wait(x + 1)

        lower = jnp.maximum(x - 1, 0)
        upper = jnp.minimum(x + 1, size_x - 1)
        mine = [low_ref[x + 1, a] for a in range(var_count)]
        below = [low_ref[x, a] for a in range(var_count)]
        above = [low_ref[x + 2, a] for a in range(var_count)]
        for b in range(var_count):
            up = pltpu.roll(contracted(lambda n: jac_ref[x, 3, n], mine, b), 1, 1)
            down = pltpu.roll(contracted(lambda n: jac_ref[x, 4, n], mine, b), size_z - 1, 1)
            total = part_ref[x, b] + contracted(lambda n: jac_ref[x, 0, n], mine, b)
            total += contracted(lambda n: jac_ref[lower, 1, n], below, b)
            total += contracted(lambda n: jac_ref[upper, 2, n], above, b)
            total += jnp.where(lane == 0, 0.0, up) + jnp.where(lane == size_z - 1, 0.0, down)
            flux_ref[x, b] = total
        return carry

    lax.fori_loop(0, size_x, plane, 0)


class Exchange:
    def __init__(self, near_count, off_count, tiles_ref, rimx_ref, rimy_ref, recv_ref, gotx_ref, goty_ref, sems):
        self.near_count, self.off_count = near_count, off_count
        self.blocks = near_count * off_count
        self.near, self.off = lax.axis_index("near"), lax.axis_index("off")
        self.me = self.near * off_count + self.off
        self.tiles, self.rimx, self.rimy = tiles_ref, rimx_ref, rimy_ref
        self.recv, self.gotx, self.goty = recv_ref, gotx_ref, goty_ref
        self.tile_send, self.tile_recv, self.rim_send, self.rim_recv, self.own = sems

    def device(self, block):
        return (block // self.off_count, lax.rem(block, self.off_count))

    def announce(self):
        barrier = pltpu.get_barrier_semaphore()

        def greet(d, carry):
            other = lax.rem(self.me + d, self.blocks)
            pl.semaphore_signal(barrier, inc=1, device_id=self.device(other), device_id_type=MESH)
            return carry

        lax.fori_loop(1, self.blocks, greet, 0)

    def meet(self):
        pl.semaphore_wait(pltpu.get_barrier_semaphore(), self.blocks - 1)

    def tile(self, d, block, slot):
        return pltpu.make_async_remote_copy(
            src_ref=self.tiles.at[block],
            dst_ref=self.recv.at[slot],
            send_sem=self.tile_send.at[d],
            recv_sem=self.tile_recv.at[d],
            device_id=self.device(block),
            device_id_type=MESH,
        )

    def own_tile(self):
        return pltpu.make_async_copy(self.tiles.at[self.me], self.recv.at[self.me], self.own)

    def rims(self):
        routes = (
            (self.rimx, self.gotx, 0, (self.near + 1, self.off), self.near < self.near_count - 1, self.near > 0),
            (self.rimx, self.gotx, 1, (self.near - 1, self.off), self.near > 0, self.near < self.near_count - 1),
            (self.rimy, self.goty, 0, (self.near, self.off + 1), self.off < self.off_count - 1, self.off > 0),
            (self.rimy, self.goty, 1, (self.near, self.off - 1), self.off > 0, self.off < self.off_count - 1),
        )
        return [
            (
                pltpu.make_async_remote_copy(
                    src_ref=source.at[i],
                    dst_ref=target.at[i],
                    send_sem=self.rim_send.at[n],
                    recv_sem=self.rim_recv.at[n],
                    device_id=device,
                    device_id_type=MESH,
                ),
                sends,
                gets,
            )
            for n, (source, target, i, device, sends, gets) in enumerate(routes)
        ]

    def send_tiles(self):
        def send(d, carry):
            self.tile(d, lax.rem(self.me + d, self.blocks), self.me).start()
            return carry

        self.own_tile().start()
        lax.fori_loop(1, self.blocks, send, 0)

    def send_rims(self):
        for copy, sends, _ in self.rims():
            pl.when(sends)(copy.start)

    def finish(self):
        def end(d, carry):
            self.tile(d, lax.rem(self.me + d, self.blocks), self.me).wait_send()
            sender = lax.rem(self.me + self.blocks - d, self.blocks)
            self.tile(d, sender, sender).wait_recv()
            return carry

        self.own_tile().wait()
        lax.fori_loop(1, self.blocks, end, 0)
        for copy, sends, gets in self.rims():
            pl.when(sends)(copy.wait_send)
            pl.when(gets)(copy.wait_recv)


def add_rims(exchange, gotx_ref, goty_ref, flux_ref):
    size_x, var_count, size_y, size_z = flux_ref.shape

    @pl.when(exchange.near > 0)
    def _():
        flux_ref[0] += gotx_ref[0]

    @pl.when(exchange.near < exchange.near_count - 1)
    def _():
        flux_ref[size_x - 1] += gotx_ref[1]

    def add(i, y):
        def plane(x, carry):
            rows = goty_ref[i, x]
            for b in range(var_count):
                flux_ref[x, b, y : y + 1, :] += rows[b : b + 1]
            return carry

        lax.fori_loop(0, size_x, plane, 0)

    @pl.when(exchange.off > 0)
    def _():
        add(0, 0)

    @pl.when(exchange.off < exchange.off_count - 1)
    def _():
        add(1, size_y - 1)


def exchange_kernel(near_count, off_count, stride, count_ref, cell_ref, owner_ref, base_ref, frac_ref, adj_ref, jac_hbm,
                    flux_ref, recv_out, side_ref, edge_ref, masked_ref, picked_ref, tiles_ref, rimx_ref, rimy_ref,
                    part_ref, jac_ref, low_ref, recv_ref, gotx_ref, goty_ref, side_sems, plane_sems, *sems):
    exchange = Exchange(near_count, off_count, tiles_ref, rimx_ref, rimy_ref, recv_ref, gotx_ref, goty_ref, sems)
    exchange.announce()
    copies = start_side(jac_hbm, side_ref, edge_ref, side_sems)
    start_planes(jac_hbm, jac_ref, plane_sems)
    tiles = pack_rows(count_ref, cell_ref, owner_ref, base_ref, frac_ref, adj_ref, masked_ref, picked_ref,
                      exchange.me, exchange.blocks, stride)
    tiles_ref[...] = tiles.reshape(exchange.blocks, 16, LANES)
    exchange.meet()
    exchange.send_tiles()
    side_flux(copies, adj_ref, side_ref, edge_ref, rimx_ref, rimy_ref, part_ref)
    exchange.send_rims()
    main_flux(adj_ref, jac_hbm, jac_ref, low_ref, part_ref, flux_ref, plane_sems)
    exchange.finish()
    add_rims(exchange, gotx_ref, goty_ref, flux_ref)
    recv_out[...] = recv_ref[...]


def overset_factors(recv_ref, stride, size_x, size_y, size_z, var_count):
    blocks = recv_ref.shape[0]
    group = LANES // stride
    mus, wxs, wys, wzs = [], [], [], []
    y_bits = size_y.bit_length() - 1

    def hat(index, fraction, length):
        at = lax.broadcasted_iota(jnp.int32, (length, LANES), 0)
        return jnp.where(at == index, 1.0 - fraction, jnp.where(at == index + 1, fraction, 0.0))

    for g in range(blocks // group):
        tile = recv_ref[g * group].astype(F32)
        for i in range(1, group):
            tile = tile + recv_ref[g * group + i].astype(F32)
        frac = tile[8:12] + tile[12:16]
        xy = tile[var_count : var_count + 1].astype(jnp.int32)
        z = tile[var_count + 1 : var_count + 2].astype(jnp.int32)
        mus.append(-tile[0:8])
        wxs.append(hat(xy >> y_bits, frac[0:1], size_x))
        wys.append(hat(xy & (size_y - 1), frac[1:2], size_y))
        wzs.append(hat(z, frac[2:3], size_z))
    return tuple(jnp.concatenate(part, axis=1) for part in (mus, wxs, wys, wzs))


def finish_kernel(stride, size_x, adj_ref, src_ref, step_ref, flux_ref, recv_ref, res_ref, upd_ref,
                  mu_ref, wx_ref, wy_ref, wz_ref, left_ref):
    planes, var_count, size_y, size_z = adj_ref.shape
    chunk = pl.program_id(0)

    @pl.when(chunk == 0)
    def _():
        mu, wx, wy, wz = overset_factors(recv_ref, stride, size_x, size_y, size_z, var_count)
        mu_ref[...] = mu
        wx_ref[...] = wx
        wy_ref[...] = wy
        wz_hi = wz.astype(BF16)
        wz_ref[0] = wz_hi
        wz_ref[1] = (wz - wz_hi.astype(F32)).astype(BF16)

    for p in range(planes):
        wxy = wy_ref[...] * wx_ref[pl.ds(chunk * planes + p, 1), :]
        for b in range(var_count):
            at = (p * var_count + b) * size_y
            left_ref[at : at + size_y, :] = (wxy * mu_ref[b : b + 1, :]).astype(BF16)
    left = left_ref[...]
    over = lax.dot_general(left, wz_ref[0], NT, preferred_element_type=F32)
    over += lax.dot_general(left, wz_ref[1], NT, preferred_element_type=F32)
    res = flux_ref[...] + over.reshape(planes, var_count, size_y, size_z) + src_ref[...]
    res_ref[...] = res
    upd_ref[...] = adj_ref[...] - step_ref[...][:, None] * res


def shards(adjoint, jacobian, source, pseudo_step, receptor_count, receptor_cell, donor_owner, donor_base, donor_fraction):
    size_x, size_y, var_count, size_z = adjoint.shape
    rows = var_count * var_count
    near_count, off_count = lax.axis_size("near"), lax.axis_size("off")
    blocks = near_count * off_count
    row_count = receptor_cell.shape[0]
    capacity = max(2, 3 * row_count // (2 * blocks))
    stride = 1 << (capacity - 1).bit_length()
    slots = blocks * stride
    vmem = pl.BlockSpec(memory_space=pltpu.VMEM)
    smem = pl.BlockSpec(memory_space=pltpu.SMEM)
    hbm = pl.BlockSpec(memory_space=pl.ANY)
    adj = jnp.transpose(adjoint, (0, 2, 1, 3))
    src = jnp.transpose(source, (0, 2, 1, 3))
    jac = jnp.transpose(jacobian, (0, 2, 3, 1, 4))
    frac = jnp.pad(donor_fraction.T, ((0, 1), (0, 0)))
    receptors = (
        receptor_count,
        receptor_cell.reshape(1, row_count),
        donor_owner.reshape(1, row_count),
        donor_base.reshape(1, row_count),
        frac,
    )
    tiles_shape = (blocks, 16, LANES)
    rimx_shape = (2, var_count, size_y, size_z)
    rimy_shape = (2, size_x, var_count, size_z)
    side_scratch = [
        pltpu.VMEM((size_x, 2, rows, size_y, size_z), BF16),
        pltpu.VMEM((2, rows, size_y, size_z), BF16),
        pltpu.VMEM((blocks * 16, row_count), BF16),
        pltpu.VMEM((var_count * size_y, row_count), F32),
    ]
    exchange_scratch = [
        pltpu.VMEM((size_x, 5, rows, size_y, size_z), BF16),
        pltpu.VMEM((size_x + 2, var_count, size_y, size_z), F32),
        pltpu.VMEM(tiles_shape, BF16),
        pltpu.VMEM(rimx_shape, F32),
        pltpu.VMEM(rimy_shape, F32),
    ]
    exchange_sems = [
        pltpu.SemaphoreType.DMA((size_x, 2)),
        pltpu.SemaphoreType.DMA((blocks,)),
        pltpu.SemaphoreType.DMA((blocks,)),
        pltpu.SemaphoreType.DMA((4,)),
        pltpu.SemaphoreType.DMA((4,)),
        pltpu.SemaphoreType.DMA,
    ]
    exchange_out = (jax.ShapeDtypeStruct(adj.shape, F32), jax.ShapeDtypeStruct(tiles_shape, BF16))
    flux, received = pl.pallas_call(
        functools.partial(exchange_kernel, near_count, off_count, stride),
        out_shape=exchange_out,
        in_specs=[smem] + [vmem] * 5 + [hbm],
        out_specs=(vmem, vmem),
        scratch_shapes=side_scratch
        + [
            pltpu.VMEM(tiles_shape, BF16),
            pltpu.VMEM(rimx_shape, F32),
            pltpu.VMEM(rimy_shape, F32),
            pltpu.VMEM(adj.shape, F32),
        ]
        + exchange_scratch
        + [pltpu.SemaphoreType.DMA((3,))]
        + exchange_sems,
        compiler_params=pltpu.CompilerParams(vmem_limit_bytes=VMEM_LIMIT, collective_id=0, has_side_effects=True),
    )(*receptors, adj, jac)
    planes = 4 if size_x % 4 == 0 else 1
    field = pl.BlockSpec((planes, var_count, size_y, size_z), lambda i: (i, 0, 0, 0))
    residual, updated = pl.pallas_call(
        functools.partial(finish_kernel, stride, size_x),
        grid=(size_x // planes,),
        out_shape=(jax.ShapeDtypeStruct(adj.shape, F32), jax.ShapeDtypeStruct(adj.shape, F32)),
        in_specs=[
            field,
            field,
            pl.BlockSpec((planes, size_y, size_z), lambda i: (i, 0, 0)),
            field,
            pl.BlockSpec(tiles_shape, lambda i: (0, 0, 0)),
        ],
        out_specs=(field, field),
        scratch_shapes=[
            pltpu.VMEM((8, slots), F32),
            pltpu.VMEM((size_x, slots), F32),
            pltpu.VMEM((size_y, slots), F32),
            pltpu.VMEM((2, size_z, slots), BF16),
            pltpu.VMEM((planes * var_count * size_y, slots), BF16),
        ],
        compiler_params=pltpu.CompilerParams(vmem_limit_bytes=VMEM_LIMIT),
    )(adj, src, pseudo_step, flux, received)
    return jnp.transpose(residual, (0, 2, 1, 3)), jnp.transpose(updated, (0, 2, 1, 3))


def solution(mesh):
    in_specs = (
        P("near", "off", None, None),
        P("near", "off", None, None, None),
        P("near", "off", None, None),
        P("near", "off", None),
        P(("near", "off")),
        P(("near", "off")),
        P(("near", "off"), None),
        P(("near", "off")),
        P(("near", "off"), None),
    )
    out_specs = (P("near", "off", None, None), P("near", "off", None, None))
    return jax.shard_map(shards, mesh=mesh, in_specs=in_specs, out_specs=out_specs, check_vma=False)
```

```python
import functools

import jax
import jax.numpy as jnp
from jax import lax
from jax.experimental import pallas as pl
from jax.experimental.pallas import tpu as pltpu
from jax.sharding import PartitionSpec as P

F32 = jnp.float32
BF16 = jnp.bfloat16
VMEM_LIMIT = 56 * 1024 * 1024
NT = (((1,), (1,)), ((), ()))
MESH = pl.DeviceIdType.MESH
LANES = 128


def contracted(blocks, values, b):
    var_count = len(values)
    total = blocks(b).astype(F32) * values[0]
    for a in range(1, var_count):
        total += blocks(a * var_count + b).astype(F32) * values[a]
    return total


def low_of(adj_ref, x):
    return [adj_ref[x, a].astype(BF16).astype(F32) for a in range(adj_ref.shape[1])]


def pack_rows(count_ref, cell_ref, owner_ref, base_ref, frac_ref, adj_ref, masked_ref, picked_ref, me, blocks, stride):
    size_x, var_count, size_y, size_z = adj_ref.shape
    rows = cell_ref.shape[1]
    z_bits = size_z.bit_length() - 1
    row = lax.broadcasted_iota(jnp.int32, (1, rows), 1)
    live = row < count_ref[0]
    cell = cell_ref[...]
    cell_z = cell & (size_z - 1)
    cell_xy = cell >> z_bits
    hot_z = jnp.where(lax.broadcasted_iota(jnp.int32, (size_z, rows), 0) == cell_z, 1.0, 0.0).astype(BF16)
    picked_ref[...] = jnp.zeros(picked_ref.shape, F32)
    y_of = lax.broadcasted_iota(jnp.int32, (size_y, rows), 0)

    planes = 4 if size_x % 4 == 0 else 1
    height = var_count * size_y

    def gather(step, carry):
        first_x = step * planes
        plane = adj_ref[pl.ds(first_x, planes)].reshape(planes * height, size_z).astype(BF16)
        found = jnp.dot(plane, hot_z, preferred_element_type=F32)
        here = [y_of == cell_xy - (first_x + p) * size_y for p in range(planes)]
        for a in range(var_count):
            at = slice(a * size_y, (a + 1) * size_y)
            chosen = picked_ref[at, :]
            for p in range(planes):
                start = p * height + a * size_y
                chosen = jnp.where(here[p], found[start : start + size_y], chosen)
            picked_ref[at, :] = chosen
        return carry

    lax.fori_loop(0, size_x // planes, gather, 0)
    base = base_ref[...]
    base_xy = (base >> z_bits).astype(F32)
    base_z = (base & (size_z - 1)).astype(F32)
    sub = lax.broadcasted_iota(jnp.int32, (8, rows), 0)
    top = jnp.where(sub == var_count, base_xy, base_z)
    for a in range(var_count):
        mu = jnp.sum(picked_ref[a * size_y : (a + 1) * size_y, :], axis=0, keepdims=True)
        top = jnp.where(sub == a, mu, top)
    axis = sub & 3
    frac = jnp.where(axis == 0, frac_ref[0:1, :], jnp.where(axis == 1, frac_ref[1:2, :], frac_ref[2:3, :]))
    frac_hi = frac.astype(BF16).astype(F32)
    payload = jnp.concatenate([top, jnp.where(sub < 4, frac_hi, frac - frac_hi)], axis=0)
    owner = jnp.where(live, owner_ref[...], -1)

    strips = rows // LANES
    block_ids = lax.broadcasted_iota(jnp.int32, (blocks, LANES), 0)
    matches = [
        jnp.where(block_ids == owner[:, s * LANES : (s + 1) * LANES], 1.0, 0.0) for s in range(strips)
    ]
    first = lax.broadcasted_iota(jnp.int32, (LANES, LANES), 0)
    second = lax.broadcasted_iota(jnp.int32, (LANES, LANES), 1)
    before = jnp.where(first < second, 1.0, 0.0).astype(BF16)
    earlier = jnp.dot(jnp.concatenate(matches, axis=0).astype(BF16), before, preferred_element_type=F32)
    carry = jnp.zeros((blocks, 1), F32)
    ranks = []
    for s in range(strips):
        here = earlier[s * blocks : (s + 1) * blocks] + carry
        ranks.append(jnp.sum(here * matches[s], axis=0, keepdims=True))
        carry = carry + jnp.sum(matches[s], axis=1, keepdims=True)
    rank = jnp.concatenate(ranks, axis=1).astype(jnp.int32)
    place = rank + lax.rem(me, LANES // stride) * stride
    hot_rank = jnp.where(lax.broadcasted_iota(jnp.int32, (LANES, rows), 0) == place, 1.0, 0.0).astype(BF16)

    def mask(o, carry):
        masked_ref[pl.ds(pl.multiple_of(o * 16, 16), 16), :] = jnp.where(owner == o, payload, 0.0).astype(BF16)
        return carry

    lax.fori_loop(0, blocks, mask, 0)
    return lax.dot_general(masked_ref[...], hot_rank, NT, preferred_element_type=F32).astype(BF16)


def start_side(jac_hbm, side_ref, edge_ref, sems):
    size_x = jac_hbm.shape[0]
    copies = [
        pltpu.make_async_copy(jac_hbm.at[size_x - 1, 1], edge_ref.at[0], sems.at[0]),
        pltpu.make_async_copy(jac_hbm.at[0, 2], edge_ref.at[1], sems.at[1]),
        pltpu.make_async_copy(jac_hbm.at[:, pl.ds(3, 2)], side_ref, sems.at[2]),
    ]
    for copy in copies:
        copy.start()
    return copies


def side_flux(copies, adj_ref, side_ref, edge_ref, rimx_ref, rimy_ref, part_ref):
    size_x, var_count, size_y, size_z = adj_ref.shape
    for copy in copies:
        copy.wait()
    for i, x in enumerate((size_x - 1, 0)):
        low = low_of(adj_ref, x)
        for b in range(var_count):
            rimx_ref[i, b] = contracted(lambda n: edge_ref[i, n], low, b)
    y_of = lax.broadcasted_iota(jnp.int32, (size_y, size_z), 0)

    def plane(x, carry):
        low = low_of(adj_ref, x)
        for b in range(var_count):
            up = pltpu.roll(contracted(lambda n: side_ref[x, 0, n], low, b), 1, 0)
            down = pltpu.roll(contracted(lambda n: side_ref[x, 1, n], low, b), size_y - 1, 0)
            rimy_ref[0, x, b : b + 1, :] = up[0:1]
            rimy_ref[1, x, b : b + 1, :] = down[size_y - 1 : size_y]
            part_ref[x, b] = jnp.where(y_of == 0, 0.0, up) + jnp.where(y_of == size_y - 1, 0.0, down)
        return carry

    lax.fori_loop(0, size_x, plane, 0)


def plane_copies(jac_hbm, jac_ref, sems, x):
    return (
        pltpu.make_async_copy(jac_hbm.at[x, pl.ds(0, 3)], jac_ref.at[x, pl.ds(0, 3)], sems.at[x, 0]),
        pltpu.make_async_copy(jac_hbm.at[x, pl.ds(5, 2)], jac_ref.at[x, pl.ds(3, 2)], sems.at[x, 1]),
    )


def start_planes(jac_hbm, jac_ref, sems):
    def start(x, carry):
        for copy in plane_copies(jac_hbm, jac_ref, sems, x):
            copy.start()
        return carry

    lax.fori_loop(0, jac_hbm.shape[0], start, 0)


def main_flux(adj_ref, jac_hbm, jac_ref, low_ref, part_ref, flux_ref, sems):
    size_x, var_count, size_y, size_z = adj_ref.shape
    low_ref[0] = jnp.zeros(low_ref.shape[1:], F32)
    low_ref[size_x + 1] = jnp.zeros(low_ref.shape[1:], F32)

    def narrow(x, carry):
        low_ref[x + 1] = adj_ref[x].astype(BF16).astype(F32)
        return carry

    lax.fori_loop(0, size_x, narrow, 0)
    lane = lax.broadcasted_iota(jnp.int32, (size_y, size_z), 1)

    def wait(x):
        for copy in plane_copies(jac_hbm, jac_ref, sems, x):
            copy.wait()

    wait(0)

    def plane(x, carry):
        @pl.when(x + 1 < size_x)
        def _():
            wait(x + 1)

        lower = jnp.maximum(x - 1, 0)
        upper = jnp.minimum(x + 1, size_x - 1)
        mine = [low_ref[x + 1, a] for a in range(var_count)]
        below = [low_ref[x, a] for a in range(var_count)]
        above = [low_ref[x + 2, a] for a in range(var_count)]
        for b in range(var_count):
            up = pltpu.roll(contracted(lambda n: jac_ref[x, 3, n], mine, b), 1, 1)
            down = pltpu.roll(contracted(lambda n: jac_ref[x, 4, n], mine, b), size_z - 1, 1)
            total = part_ref[x, b] + contracted(lambda n: jac_ref[x, 0, n], mine, b)
            total += contracted(lambda n: jac_ref[lower, 1, n], below, b)
            total += contracted(lambda n: jac_ref[upper, 2, n], above, b)
            total += jnp.where(lane == 0, 0.0, up) + jnp.where(lane == size_z - 1, 0.0, down)
            flux_ref[x, b] = total
        return carry

    lax.fori_loop(0, size_x, plane, 0)


class Exchange:
    def __init__(self, near_count, off_count, tiles_ref, rimx_ref, rimy_ref, recv_ref, gotx_ref, goty_ref, sems):
        self.near_count, self.off_count = near_count, off_count
        self.blocks = near_count * off_count
        self.near, self.off = lax.axis_index("near"), lax.axis_index("off")
        self.me = self.near * off_count + self.off
        self.tiles, self.rimx, self.rimy = tiles_ref, rimx_ref, rimy_ref
        self.recv, self.gotx, self.goty = recv_ref, gotx_ref, goty_ref
        self.tile_send, self.tile_recv, self.rim_send, self.rim_recv, self.own = sems

    def device(self, block):
        return (block // self.off_count, lax.rem(block, self.off_count))

    def announce(self):
        barrier = pltpu.get_barrier_semaphore()

        def greet(d, carry):
            other = lax.rem(self.me + d, self.blocks)
            pl.semaphore_signal(barrier, inc=1, device_id=self.device(other), device_id_type=MESH)
            return carry

        lax.fori_loop(1, self.blocks, greet, 0)

    def meet(self):
        pl.semaphore_wait(pltpu.get_barrier_semaphore(), self.blocks - 1)

    def tile(self, d, block, slot):
        return pltpu.make_async_remote_copy(
            src_ref=self.tiles.at[block],
            dst_ref=self.recv.at[slot],
            send_sem=self.tile_send.at[d],
            recv_sem=self.tile_recv.at[d],
            device_id=self.device(block),
            device_id_type=MESH,
        )

    def own_tile(self):
        return pltpu.make_async_copy(self.tiles.at[self.me], self.recv.at[self.me], self.own)

    def rims(self):
        routes = (
            (self.rimx, self.gotx, 0, (self.near + 1, self.off), self.near < self.near_count - 1, self.near > 0),
            (self.rimx, self.gotx, 1, (self.near - 1, self.off), self.near > 0, self.near < self.near_count - 1),
            (self.rimy, self.goty, 0, (self.near, self.off + 1), self.off < self.off_count - 1, self.off > 0),
            (self.rimy, self.goty, 1, (self.near, self.off - 1), self.off > 0, self.off < self.off_count - 1),
        )
        return [
            (
                pltpu.make_async_remote_copy(
                    src_ref=source.at[i],
                    dst_ref=target.at[i],
                    send_sem=self.rim_send.at[n],
                    recv_sem=self.rim_recv.at[n],
                    device_id=device,
                    device_id_type=MESH,
                ),
                sends,
                gets,
            )
            for n, (source, target, i, device, sends, gets) in enumerate(routes)
        ]

    def send_tiles(self):
        def send(d, carry):
            self.tile(d, lax.rem(self.me + d, self.blocks), self.me).start()
            return carry

        self.own_tile().start()
        lax.fori_loop(1, self.blocks, send, 0)

    def send_rims(self):
        for copy, sends, _ in self.rims():
            pl.when(sends)(copy.start)

    def finish(self):
        def end(d, carry):
            self.tile(d, lax.rem(self.me + d, self.blocks), self.me).wait_send()
            sender = lax.rem(self.me + self.blocks - d, self.blocks)
            self.tile(d, sender, sender).wait_recv()
            return carry

        self.own_tile().wait()
        lax.fori_loop(1, self.blocks, end, 0)
        for copy, sends, gets in self.rims():
            pl.when(sends)(copy.wait_send)
            pl.when(gets)(copy.wait_recv)


def add_rims(exchange, gotx_ref, goty_ref, flux_ref):
    size_x, var_count, size_y, size_z = flux_ref.shape

    @pl.when(exchange.near > 0)
    def _():
        flux_ref[0] += gotx_ref[0]

    @pl.when(exchange.near < exchange.near_count - 1)
    def _():
        flux_ref[size_x - 1] += gotx_ref[1]

    def add(i, y):
        def plane(x, carry):
            rows = goty_ref[i, x]
            for b in range(var_count):
                flux_ref[x, b, y : y + 1, :] += rows[b : b + 1]
            return carry

        lax.fori_loop(0, size_x, plane, 0)

    @pl.when(exchange.off > 0)
    def _():
        add(0, 0)

    @pl.when(exchange.off < exchange.off_count - 1)
    def _():
        add(1, size_y - 1)


def exchange_kernel(near_count, off_count, stride, count_ref, cell_ref, owner_ref, base_ref, frac_ref, adj_ref, jac_hbm,
                    flux_ref, recv_out, side_ref, edge_ref, masked_ref, picked_ref, tiles_ref, rimx_ref, rimy_ref,
                    part_ref, jac_ref, low_ref, recv_ref, gotx_ref, goty_ref, side_sems, plane_sems, *sems):
    exchange = Exchange(near_count, off_count, tiles_ref, rimx_ref, rimy_ref, recv_ref, gotx_ref, goty_ref, sems)
    exchange.announce()
    copies = start_side(jac_hbm, side_ref, edge_ref, side_sems)
    start_planes(jac_hbm, jac_ref, plane_sems)
    tiles = pack_rows(count_ref, cell_ref, owner_ref, base_ref, frac_ref, adj_ref, masked_ref, picked_ref,
                      exchange.me, exchange.blocks, stride)
    tiles_ref[...] = tiles.reshape(exchange.blocks, 16, LANES)
    exchange.meet()
    exchange.send_tiles()
    side_flux(copies, adj_ref, side_ref, edge_ref, rimx_ref, rimy_ref, part_ref)
    exchange.send_rims()
    main_flux(adj_ref, jac_hbm, jac_ref, low_ref, part_ref, flux_ref, plane_sems)
    exchange.finish()
    add_rims(exchange, gotx_ref, goty_ref, flux_ref)
    recv_out[...] = recv_ref[...]


def overset_factors(recv_ref, stride, size_x, size_y, size_z, var_count):
    blocks = recv_ref.shape[0]
    group = LANES // stride
    mus, wxs, wys, wzs = [], [], [], []
    y_bits = size_y.bit_length() - 1

    def hat(index, fraction, length):
        at = lax.broadcasted_iota(jnp.int32, (length, LANES), 0)
        return jnp.where(at == index, 1.0 - fraction, jnp.where(at == index + 1, fraction, 0.0))

    for g in range(blocks // group):
        tile = recv_ref[g * group].astype(F32)
        for i in range(1, group):
            tile = tile + recv_ref[g * group + i].astype(F32)
        frac = tile[8:12] + tile[12:16]
        xy = tile[var_count : var_count + 1].astype(jnp.int32)
        z = tile[var_count + 1 : var_count + 2].astype(jnp.int32)
        mus.append(-tile[0:8])
        wxs.append(hat(xy >> y_bits, frac[0:1], size_x))
        wys.append(hat(xy & (size_y - 1), frac[1:2], size_y))
        wzs.append(hat(z, frac[2:3], size_z))
    return tuple(jnp.concatenate(part, axis=1) for part in (mus, wxs, wys, wzs))


def finish_kernel(stride, size_x, adj_ref, src_ref, step_ref, flux_ref, recv_ref, res_ref, upd_ref,
                  mu_ref, wx_ref, wy_ref, wz_ref):
    planes, var_count, size_y, size_z = adj_ref.shape
    chunk = pl.program_id(0)

    @pl.when(chunk == 0)
    def _():
        mu, wx, wy, wz = overset_factors(recv_ref, stride, size_x, size_y, size_z, var_count)
        mu_ref[...] = mu
        wx_ref[...] = wx
        wy_ref[...] = wy
        wz_hi = wz.astype(BF16)
        wz_ref[0:size_z, :] = wz_hi
        wz_ref[size_z : 2 * size_z, :] = (wz - wz_hi.astype(F32)).astype(BF16)

    slots = wz_ref.shape[1]
    width = min(slots, 2 * LANES)
    both = jnp.zeros((planes * var_count * size_y, 2 * size_z), F32)
    for k in range(0, slots, width):
        at = slice(k, k + width)
        left = []
        for p in range(planes):
            wxy = wy_ref[:, at] * wx_ref[pl.ds(chunk * planes + p, 1), at]
            left += [(wxy * mu_ref[b : b + 1, at]).astype(BF16) for b in range(var_count)]
        both += lax.dot_general(jnp.concatenate(left, axis=0), wz_ref[:, at], NT, preferred_element_type=F32)
    over = both[:, 0:size_z] + both[:, size_z : 2 * size_z]
    res = flux_ref[...] + over.reshape(planes, var_count, size_y, size_z) + src_ref[...]
    res_ref[...] = res
    upd_ref[...] = adj_ref[...] - step_ref[...][:, None] * res


def shards(adjoint, jacobian, source, pseudo_step, receptor_count, receptor_cell, donor_owner, donor_base, donor_fraction):
    size_x, size_y, var_count, size_z = adjoint.shape
    rows = var_count * var_count
    near_count, off_count = lax.axis_size("near"), lax.axis_size("off")
    blocks = near_count * off_count
    row_count = receptor_cell.shape[0]
    capacity = max(2, 3 * row_count // (2 * blocks))
    stride = 1 << (capacity - 1).bit_length()
    slots = blocks * stride
    vmem = pl.BlockSpec(memory_space=pltpu.VMEM)
    smem = pl.BlockSpec(memory_space=pltpu.SMEM)
    hbm = pl.BlockSpec(memory_space=pl.ANY)
    adj = jnp.transpose(adjoint, (0, 2, 1, 3))
    src = jnp.transpose(source, (0, 2, 1, 3))
    jac = jnp.transpose(jacobian, (0, 2, 3, 1, 4))
    receptors = (
        receptor_count,
        receptor_cell.reshape(1, row_count),
        donor_owner.reshape(1, row_count),
        donor_base.reshape(1, row_count),
        donor_fraction.T,
    )
    tiles_shape = (blocks, 16, LANES)
    rimx_shape = (2, var_count, size_y, size_z)
    rimy_shape = (2, size_x, var_count, size_z)
    side_scratch = [
        pltpu.VMEM((size_x, 2, rows, size_y, size_z), BF16),
        pltpu.VMEM((2, rows, size_y, size_z), BF16),
        pltpu.VMEM((blocks * 16, row_count), BF16),
        pltpu.VMEM((var_count * size_y, row_count), F32),
    ]
    exchange_scratch = [
        pltpu.VMEM((size_x, 5, rows, size_y, size_z), BF16),
        pltpu.VMEM((size_x + 2, var_count, size_y, size_z), F32),
        pltpu.VMEM(tiles_shape, BF16),
        pltpu.VMEM(rimx_shape, F32),
        pltpu.VMEM(rimy_shape, F32),
    ]
    exchange_sems = [
        pltpu.SemaphoreType.DMA((size_x, 2)),
        pltpu.SemaphoreType.DMA((blocks,)),
        pltpu.SemaphoreType.DMA((blocks,)),
        pltpu.SemaphoreType.DMA((4,)),
        pltpu.SemaphoreType.DMA((4,)),
        pltpu.SemaphoreType.DMA,
    ]
    exchange_out = (jax.ShapeDtypeStruct(adj.shape, F32), jax.ShapeDtypeStruct(tiles_shape, BF16))
    flux, received = pl.pallas_call(
        functools.partial(exchange_kernel, near_count, off_count, stride),
        out_shape=exchange_out,
        in_specs=[smem] + [vmem] * 5 + [hbm],
        out_specs=(vmem, vmem),
        scratch_shapes=side_scratch
        + [
            pltpu.VMEM(tiles_shape, BF16),
            pltpu.VMEM(rimx_shape, F32),
            pltpu.VMEM(rimy_shape, F32),
            pltpu.VMEM(adj.shape, F32),
        ]
        + exchange_scratch
        + [pltpu.SemaphoreType.DMA((3,))]
        + exchange_sems,
        compiler_params=pltpu.CompilerParams(vmem_limit_bytes=VMEM_LIMIT, collective_id=0, has_side_effects=True),
    )(*receptors, adj, jac)
    planes = 4 if size_x % 4 == 0 else 1
    field = pl.BlockSpec((planes, var_count, size_y, size_z), lambda i: (i, 0, 0, 0))
    residual, updated = pl.pallas_call(
        functools.partial(finish_kernel, stride, size_x),
        grid=(size_x // planes,),
        out_shape=(jax.ShapeDtypeStruct(adj.shape, F32), jax.ShapeDtypeStruct(adj.shape, F32)),
        in_specs=[
            field,
            field,
            pl.BlockSpec((planes, size_y, size_z), lambda i: (i, 0, 0)),
            field,
            pl.BlockSpec(tiles_shape, lambda i: (0, 0, 0)),
        ],
        out_specs=(field, field),
        scratch_shapes=[
            pltpu.VMEM((8, slots), F32),
            pltpu.VMEM((size_x, slots), F32),
            pltpu.VMEM((size_y, slots), F32),
            pltpu.VMEM((2 * size_z, slots), BF16),
        ],
        compiler_params=pltpu.CompilerParams(vmem_limit_bytes=VMEM_LIMIT),
    )(adj, src, pseudo_step, flux, received)
    return jnp.transpose(residual, (0, 2, 1, 3)), jnp.transpose(updated, (0, 2, 1, 3))


def solution(mesh):
    in_specs = (
        P("near", "off", None, None),
        P("near", "off", None, None, None),
        P("near", "off", None, None),
        P("near", "off", None),
        P(("near", "off")),
        P(("near", "off")),
        P(("near", "off"), None),
        P(("near", "off")),
        P(("near", "off"), None),
    )
    out_specs = (P("near", "off", None, None), P("near", "off", None, None))
    return jax.shard_map(shards, mesh=mesh, in_specs=in_specs, out_specs=out_specs, check_vma=False)
```

```python
import functools

import jax
import jax.numpy as jnp
from jax import lax
from jax.experimental import pallas as pl
from jax.experimental.pallas import tpu as pltpu
from jax.sharding import PartitionSpec as P

F32 = jnp.float32
BF16 = jnp.bfloat16
VMEM_LIMIT = 56 * 1024 * 1024
NT = (((1,), (1,)), ((), ()))
MESH = pl.DeviceIdType.MESH
LANES = 128


def contracted(blocks, values, b):
    var_count = len(values)
    total = blocks(b).astype(F32) * values[0]
    for a in range(1, var_count):
        total += blocks(a * var_count + b).astype(F32) * values[a]
    return total


def low_of(adj_ref, x):
    return [adj_ref[x, a].astype(BF16).astype(F32) for a in range(adj_ref.shape[1])]


def pack_rows(count_ref, cell_ref, owner_ref, base_ref, frac_ref, adj_ref, masked_ref, picked_ref, me, blocks, stride):
    size_x, var_count, size_y, size_z = adj_ref.shape
    rows = cell_ref.shape[1]
    z_bits = size_z.bit_length() - 1
    row = lax.broadcasted_iota(jnp.int32, (1, rows), 1)
    live = row < count_ref[0]
    cell = cell_ref[...]
    cell_z = cell & (size_z - 1)
    cell_xy = cell >> z_bits
    hot_z = jnp.where(lax.broadcasted_iota(jnp.int32, (size_z, rows), 0) == cell_z, 1.0, 0.0).astype(BF16)
    picked_ref[...] = jnp.zeros(picked_ref.shape, F32)
    y_of = lax.broadcasted_iota(jnp.int32, (size_y, rows), 0)

    planes = 4 if size_x % 4 == 0 else 1
    height = var_count * size_y

    def gather(step, carry):
        first_x = step * planes
        plane = adj_ref[pl.ds(first_x, planes)].reshape(planes * height, size_z).astype(BF16)
        found = jnp.dot(plane, hot_z, preferred_element_type=F32)
        here = [y_of == cell_xy - (first_x + p) * size_y for p in range(planes)]
        for a in range(var_count):
            at = slice(a * size_y, (a + 1) * size_y)
            chosen = picked_ref[at, :]
            for p in range(planes):
                start = p * height + a * size_y
                chosen = jnp.where(here[p], found[start : start + size_y], chosen)
            picked_ref[at, :] = chosen
        return carry

    lax.fori_loop(0, size_x // planes, gather, 0)
    base = base_ref[...]
    base_xy = (base >> z_bits).astype(F32)
    base_z = (base & (size_z - 1)).astype(F32)
    sub = lax.broadcasted_iota(jnp.int32, (8, rows), 0)
    top = jnp.where(sub == var_count, base_xy, base_z)
    for a in range(var_count):
        mu = jnp.sum(picked_ref[a * size_y : (a + 1) * size_y, :], axis=0, keepdims=True)
        top = jnp.where(sub == a, mu, top)
    axis = sub & 3
    frac = jnp.where(axis == 0, frac_ref[0:1, :], jnp.where(axis == 1, frac_ref[1:2, :], frac_ref[2:3, :]))
    frac_hi = frac.astype(BF16).astype(F32)
    payload = jnp.concatenate([top, jnp.where(sub < 4, frac_hi, frac - frac_hi)], axis=0)
    owner = jnp.where(live, owner_ref[...], -1)

    strips = rows // LANES
    block_ids = lax.broadcasted_iota(jnp.int32, (blocks, LANES), 0)
    matches = [
        jnp.where(block_ids == owner[:, s * LANES : (s + 1) * LANES], 1.0, 0.0) for s in range(strips)
    ]
    first = lax.broadcasted_iota(jnp.int32, (LANES, LANES), 0)
    second = lax.broadcasted_iota(jnp.int32, (LANES, LANES), 1)
    before = jnp.where(first < second, 1.0, 0.0).astype(BF16)
    earlier = jnp.dot(jnp.concatenate(matches, axis=0).astype(BF16), before, preferred_element_type=F32)
    carry = jnp.zeros((blocks, 1), F32)
    ranks = []
    for s in range(strips):
        here = earlier[s * blocks : (s + 1) * blocks] + carry
        ranks.append(jnp.sum(here * matches[s], axis=0, keepdims=True))
        carry = carry + jnp.sum(matches[s], axis=1, keepdims=True)
    rank = jnp.concatenate(ranks, axis=1).astype(jnp.int32)
    place = rank + lax.rem(me, LANES // stride) * stride
    hot_rank = jnp.where(lax.broadcasted_iota(jnp.int32, (LANES, rows), 0) == place, 1.0, 0.0).astype(BF16)

    def mask(o, carry):
        masked_ref[pl.ds(pl.multiple_of(o * 16, 16), 16), :] = jnp.where(owner == o, payload, 0.0).astype(BF16)
        return carry

    lax.fori_loop(0, blocks, mask, 0, unroll=4)
    return lax.dot_general(masked_ref[...], hot_rank, NT, preferred_element_type=F32).astype(BF16)


def start_side(jac_hbm, side_ref, edge_ref, sems):
    size_x = jac_hbm.shape[0]
    copies = [
        pltpu.make_async_copy(jac_hbm.at[size_x - 1, 1], edge_ref.at[0], sems.at[0]),
        pltpu.make_async_copy(jac_hbm.at[0, 2], edge_ref.at[1], sems.at[1]),
        pltpu.make_async_copy(jac_hbm.at[:, pl.ds(3, 2)], side_ref, sems.at[2]),
    ]
    for copy in copies:
        copy.start()
    return copies


def side_flux(copies, adj_ref, side_ref, edge_ref, rimx_ref, rimy_ref, part_ref):
    size_x, var_count, size_y, size_z = adj_ref.shape
    for copy in copies:
        copy.wait()
    for i, x in enumerate((size_x - 1, 0)):
        low = low_of(adj_ref, x)
        for b in range(var_count):
            rimx_ref[i, b] = contracted(lambda n: edge_ref[i, n], low, b)
    y_of = lax.broadcasted_iota(jnp.int32, (size_y, size_z), 0)

    def plane(x, carry):
        low = low_of(adj_ref, x)
        for b in range(var_count):
            up = pltpu.roll(contracted(lambda n: side_ref[x, 0, n], low, b), 1, 0)
            down = pltpu.roll(contracted(lambda n: side_ref[x, 1, n], low, b), size_y - 1, 0)
            rimy_ref[0, x, b : b + 1, :] = up[0:1]
            rimy_ref[1, x, b : b + 1, :] = down[size_y - 1 : size_y]
            part_ref[x, b] = jnp.where(y_of == 0, 0.0, up) + jnp.where(y_of == size_y - 1, 0.0, down)
        return carry

    lax.fori_loop(0, size_x, plane, 0)


def plane_copies(jac_hbm, jac_ref, sems, x):
    return (
        pltpu.make_async_copy(jac_hbm.at[x, pl.ds(0, 3)], jac_ref.at[x, pl.ds(0, 3)], sems.at[x, 0]),
        pltpu.make_async_copy(jac_hbm.at[x, pl.ds(5, 2)], jac_ref.at[x, pl.ds(3, 2)], sems.at[x, 1]),
    )


def start_planes(jac_hbm, jac_ref, sems):
    def start(x, carry):
        for copy in plane_copies(jac_hbm, jac_ref, sems, x):
            copy.start()
        return carry

    lax.fori_loop(0, jac_hbm.shape[0], start, 0)


def main_flux(adj_ref, jac_hbm, jac_ref, low_ref, part_ref, flux_ref, sems):
    size_x, var_count, size_y, size_z = adj_ref.shape
    low_ref[0] = jnp.zeros(low_ref.shape[1:], F32)
    low_ref[size_x + 1] = jnp.zeros(low_ref.shape[1:], F32)

    def narrow(x, carry):
        low_ref[x + 1] = adj_ref[x].astype(BF16).astype(F32)
        return carry

    lax.fori_loop(0, size_x, narrow, 0)
    lane = lax.broadcasted_iota(jnp.int32, (size_y, size_z), 1)

    def wait(x):
        for copy in plane_copies(jac_hbm, jac_ref, sems, x):
            copy.wait()

    wait(0)

    def plane(x, carry):
        @pl.when(x + 1 < size_x)
        def _():
            wait(x + 1)

        lower = jnp.maximum(x - 1, 0)
        upper = jnp.minimum(x + 1, size_x - 1)
        mine = [low_ref[x + 1, a] for a in range(var_count)]
        below = [low_ref[x, a] for a in range(var_count)]
        above = [low_ref[x + 2, a] for a in range(var_count)]
        for b in range(var_count):
            up = pltpu.roll(contracted(lambda n: jac_ref[x, 3, n], mine, b), 1, 1)
            down = pltpu.roll(contracted(lambda n: jac_ref[x, 4, n], mine, b), size_z - 1, 1)
            total = part_ref[x, b] + contracted(lambda n: jac_ref[x, 0, n], mine, b)
            total += contracted(lambda n: jac_ref[lower, 1, n], below, b)
            total += contracted(lambda n: jac_ref[upper, 2, n], above, b)
            total += jnp.where(lane == 0, 0.0, up) + jnp.where(lane == size_z - 1, 0.0, down)
            flux_ref[x, b] = total
        return carry

    lax.fori_loop(0, size_x, plane, 0)


class Exchange:
    def __init__(self, near_count, off_count, tiles_ref, rimx_ref, rimy_ref, recv_ref, gotx_ref, goty_ref, sems):
        self.near_count, self.off_count = near_count, off_count
        self.blocks = near_count * off_count
        self.near, self.off = lax.axis_index("near"), lax.axis_index("off")
        self.me = self.near * off_count + self.off
        self.tiles, self.rimx, self.rimy = tiles_ref, rimx_ref, rimy_ref
        self.recv, self.gotx, self.goty = recv_ref, gotx_ref, goty_ref
        self.tile_send, self.tile_recv, self.rim_send, self.rim_recv, self.own = sems

    def device(self, block):
        return (block // self.off_count, lax.rem(block, self.off_count))

    def announce(self):
        barrier = pltpu.get_barrier_semaphore()

        def greet(d, carry):
            other = lax.rem(self.me + d, self.blocks)
            pl.semaphore_signal(barrier, inc=1, device_id=self.device(other), device_id_type=MESH)
            return carry

        lax.fori_loop(1, self.blocks, greet, 0)

    def meet(self):
        pl.semaphore_wait(pltpu.get_barrier_semaphore(), self.blocks - 1)

    def tile(self, d, block, slot):
        return pltpu.make_async_remote_copy(
            src_ref=self.tiles.at[block],
            dst_ref=self.recv.at[slot],
            send_sem=self.tile_send.at[d],
            recv_sem=self.tile_recv.at[d],
            device_id=self.device(block),
            device_id_type=MESH,
        )

    def own_tile(self):
        return pltpu.make_async_copy(self.tiles.at[self.me], self.recv.at[self.me], self.own)

    def rims(self):
        routes = (
            (self.rimx, self.gotx, 0, (self.near + 1, self.off), self.near < self.near_count - 1, self.near > 0),
            (self.rimx, self.gotx, 1, (self.near - 1, self.off), self.near > 0, self.near < self.near_count - 1),
            (self.rimy, self.goty, 0, (self.near, self.off + 1), self.off < self.off_count - 1, self.off > 0),
            (self.rimy, self.goty, 1, (self.near, self.off - 1), self.off > 0, self.off < self.off_count - 1),
        )
        return [
            (
                pltpu.make_async_remote_copy(
                    src_ref=source.at[i],
                    dst_ref=target.at[i],
                    send_sem=self.rim_send.at[n],
                    recv_sem=self.rim_recv.at[n],
                    device_id=device,
                    device_id_type=MESH,
                ),
                sends,
                gets,
            )
            for n, (source, target, i, device, sends, gets) in enumerate(routes)
        ]

    def send_tiles(self):
        def send(d, carry):
            self.tile(d, lax.rem(self.me + d, self.blocks), self.me).start()
            return carry

        self.own_tile().start()
        lax.fori_loop(1, self.blocks, send, 0)

    def send_rims(self):
        for copy, sends, _ in self.rims():
            pl.when(sends)(copy.start)

    def finish(self):
        def end(d, carry):
            self.tile(d, lax.rem(self.me + d, self.blocks), self.me).wait_send()
            sender = lax.rem(self.me + self.blocks - d, self.blocks)
            self.tile(d, sender, sender).wait_recv()
            return carry

        self.own_tile().wait()
        lax.fori_loop(1, self.blocks, end, 0)
        for copy, sends, gets in self.rims():
            pl.when(sends)(copy.wait_send)
            pl.when(gets)(copy.wait_recv)


def add_rims(exchange, gotx_ref, goty_ref, flux_ref):
    size_x, var_count, size_y, size_z = flux_ref.shape

    @pl.when(exchange.near > 0)
    def _():
        flux_ref[0] += gotx_ref[0]

    @pl.when(exchange.near < exchange.near_count - 1)
    def _():
        flux_ref[size_x - 1] += gotx_ref[1]

    def add(i, y):
        def plane(x, carry):
            rows = goty_ref[i, x]
            for b in range(var_count):
                flux_ref[x, b, y : y + 1, :] += rows[b : b + 1]
            return carry

        lax.fori_loop(0, size_x, plane, 0)

    @pl.when(exchange.off > 0)
    def _():
        add(0, 0)

    @pl.when(exchange.off < exchange.off_count - 1)
    def _():
        add(1, size_y - 1)


def exchange_kernel(near_count, off_count, stride, count_ref, cell_ref, owner_ref, base_ref, frac_ref, adj_ref, jac_hbm,
                    flux_ref, recv_out, side_ref, edge_ref, masked_ref, picked_ref, tiles_ref, rimx_ref, rimy_ref,
                    part_ref, jac_ref, low_ref, recv_ref, gotx_ref, goty_ref, side_sems, plane_sems, *sems):
    exchange = Exchange(near_count, off_count, tiles_ref, rimx_ref, rimy_ref, recv_ref, gotx_ref, goty_ref, sems)
    exchange.announce()
    copies = start_side(jac_hbm, side_ref, edge_ref, side_sems)
    start_planes(jac_hbm, jac_ref, plane_sems)
    tiles = pack_rows(count_ref, cell_ref, owner_ref, base_ref, frac_ref, adj_ref, masked_ref, picked_ref,
                      exchange.me, exchange.blocks, stride)
    tiles_ref[...] = tiles.reshape(exchange.blocks, 16, LANES)
    exchange.meet()
    exchange.send_tiles()
    side_flux(copies, adj_ref, side_ref, edge_ref, rimx_ref, rimy_ref, part_ref)
    exchange.send_rims()
    main_flux(adj_ref, jac_hbm, jac_ref, low_ref, part_ref, flux_ref, plane_sems)
    exchange.finish()
    add_rims(exchange, gotx_ref, goty_ref, flux_ref)
    recv_out[...] = recv_ref[...]


def overset_factors(recv_ref, stride, size_x, size_y, size_z, var_count):
    blocks = recv_ref.shape[0]
    group = LANES // stride
    mus, wxs, wys, wzs = [], [], [], []
    y_bits = size_y.bit_length() - 1

    def hat(index, fraction, length):
        at = lax.broadcasted_iota(jnp.int32, (length, LANES), 0)
        return jnp.where(at == index, 1.0 - fraction, jnp.where(at == index + 1, fraction, 0.0))

    for g in range(blocks // group):
        tile = recv_ref[g * group].astype(F32)
        for i in range(1, group):
            tile = tile + recv_ref[g * group + i].astype(F32)
        frac = tile[8:12] + tile[12:16]
        xy = tile[var_count : var_count + 1].astype(jnp.int32)
        z = tile[var_count + 1 : var_count + 2].astype(jnp.int32)
        mus.append(-tile[0:8])
        wxs.append(hat(xy >> y_bits, frac[0:1], size_x))
        wys.append(hat(xy & (size_y - 1), frac[1:2], size_y))
        wzs.append(hat(z, frac[2:3], size_z).T)
    return tuple(jnp.concatenate(part, axis=1) for part in (mus, wxs, wys)) + (jnp.concatenate(wzs, axis=0),)


def finish_kernel(stride, size_x, adj_ref, src_ref, step_ref, flux_ref, recv_ref, res_ref, upd_ref,
                  mu_ref, wx_ref, wy_ref, wz_ref):
    planes, var_count, size_y, size_z = adj_ref.shape
    chunk = pl.program_id(0)

    @pl.when(chunk == 0)
    def _():
        mu, wx, wy, wz = overset_factors(recv_ref, stride, size_x, size_y, size_z, var_count)
        mu_ref[...] = mu
        wx_ref[...] = wx
        wy_ref[...] = wy
        wz_hi = wz.astype(BF16)
        wz_ref[:, 0:size_z] = wz_hi
        wz_ref[:, size_z : 2 * size_z] = (wz - wz_hi.astype(F32)).astype(BF16)

    slots = wz_ref.shape[0]
    width = min(slots, 2 * LANES)
    both = jnp.zeros((planes * var_count * size_y, 2 * size_z), F32)
    for k in range(0, slots, width):
        at = slice(k, k + width)
        left = []
        for p in range(planes):
            wxy = wy_ref[:, at] * wx_ref[pl.ds(chunk * planes + p, 1), at]
            left += [(wxy * mu_ref[b : b + 1, at]).astype(BF16) for b in range(var_count)]
        both += jnp.dot(jnp.concatenate(left, axis=0), wz_ref[at, :], preferred_element_type=F32)
    over = both[:, 0:size_z] + both[:, size_z : 2 * size_z]
    res = flux_ref[...] + over.reshape(planes, var_count, size_y, size_z) + src_ref[...]
    res_ref[...] = res
    upd_ref[...] = adj_ref[...] - step_ref[...][:, None] * res


def shards(adjoint, jacobian, source, pseudo_step, receptor_count, receptor_cell, donor_owner, donor_base, donor_fraction):
    size_x, size_y, var_count, size_z = adjoint.shape
    rows = var_count * var_count
    near_count, off_count = lax.axis_size("near"), lax.axis_size("off")
    blocks = near_count * off_count
    row_count = receptor_cell.shape[0]
    capacity = max(2, 3 * row_count // (2 * blocks))
    stride = 1 << (capacity - 1).bit_length()
    slots = blocks * stride
    vmem = pl.BlockSpec(memory_space=pltpu.VMEM)
    smem = pl.BlockSpec(memory_space=pltpu.SMEM)
    hbm = pl.BlockSpec(memory_space=pl.ANY)
    adj = jnp.transpose(adjoint, (0, 2, 1, 3))
    src = jnp.transpose(source, (0, 2, 1, 3))
    jac = jnp.transpose(jacobian, (0, 2, 3, 1, 4))
    receptors = (
        receptor_count,
        receptor_cell.reshape(1, row_count),
        donor_owner.reshape(1, row_count),
        donor_base.reshape(1, row_count),
        donor_fraction.T,
    )
    tiles_shape = (blocks, 16, LANES)
    rimx_shape = (2, var_count, size_y, size_z)
    rimy_shape = (2, size_x, var_count, size_z)
    side_scratch = [
        pltpu.VMEM((size_x, 2, rows, size_y, size_z), BF16),
        pltpu.VMEM((2, rows, size_y, size_z), BF16),
        pltpu.VMEM((blocks * 16, row_count), BF16),
        pltpu.VMEM((var_count * size_y, row_count), F32),
    ]
    exchange_scratch = [
        pltpu.VMEM((size_x, 5, rows, size_y, size_z), BF16),
        pltpu.VMEM((size_x + 2, var_count, size_y, size_z), F32),
        pltpu.VMEM(tiles_shape, BF16),
        pltpu.VMEM(rimx_shape, F32),
        pltpu.VMEM(rimy_shape, F32),
    ]
    exchange_sems = [
        pltpu.SemaphoreType.DMA((size_x, 2)),
        pltpu.SemaphoreType.DMA((blocks,)),
        pltpu.SemaphoreType.DMA((blocks,)),
        pltpu.SemaphoreType.DMA((4,)),
        pltpu.SemaphoreType.DMA((4,)),
        pltpu.SemaphoreType.DMA,
    ]
    exchange_out = (jax.ShapeDtypeStruct(adj.shape, F32), jax.ShapeDtypeStruct(tiles_shape, BF16))
    flux, received = pl.pallas_call(
        functools.partial(exchange_kernel, near_count, off_count, stride),
        out_shape=exchange_out,
        in_specs=[smem] + [vmem] * 5 + [hbm],
        out_specs=(vmem, vmem),
        scratch_shapes=side_scratch
        + [
            pltpu.VMEM(tiles_shape, BF16),
            pltpu.VMEM(rimx_shape, F32),
            pltpu.VMEM(rimy_shape, F32),
            pltpu.VMEM(adj.shape, F32),
        ]
        + exchange_scratch
        + [pltpu.SemaphoreType.DMA((3,))]
        + exchange_sems,
        compiler_params=pltpu.CompilerParams(vmem_limit_bytes=VMEM_LIMIT, collective_id=0, has_side_effects=True),
    )(*receptors, adj, jac)
    planes = 4 if size_x % 4 == 0 else 1
    field = pl.BlockSpec((planes, var_count, size_y, size_z), lambda i: (i, 0, 0, 0))
    residual, updated = pl.pallas_call(
        functools.partial(finish_kernel, stride, size_x),
        grid=(size_x // planes,),
        out_shape=(jax.ShapeDtypeStruct(adj.shape, F32), jax.ShapeDtypeStruct(adj.shape, F32)),
        in_specs=[
            field,
            field,
            pl.BlockSpec((planes, size_y, size_z), lambda i: (i, 0, 0)),
            field,
            pl.BlockSpec(tiles_shape, lambda i: (0, 0, 0)),
        ],
        out_specs=(field, field),
        scratch_shapes=[
            pltpu.VMEM((8, slots), F32),
            pltpu.VMEM((size_x, slots), F32),
            pltpu.VMEM((size_y, slots), F32),
            pltpu.VMEM((slots, 2 * size_z), BF16),
        ],
        compiler_params=pltpu.CompilerParams(vmem_limit_bytes=VMEM_LIMIT),
    )(adj, src, pseudo_step, flux, received)
    return jnp.transpose(residual, (0, 2, 1, 3)), jnp.transpose(updated, (0, 2, 1, 3))


def solution(mesh):
    in_specs = (
        P("near", "off", None, None),
        P("near", "off", None, None, None),
        P("near", "off", None, None),
        P("near", "off", None),
        P(("near", "off")),
        P(("near", "off")),
        P(("near", "off"), None),
        P(("near", "off")),
        P(("near", "off"), None),
    )
    out_specs = (P("near", "off", None, None), P("near", "off", None, None))
    return jax.shard_map(shards, mesh=mesh, in_specs=in_specs, out_specs=out_specs, check_vma=False)
```
